32 devices in a mesh: row: 8 (over z, y), col: 4 (over x, core).
Axes of the slice: x: 2, y: 2, z: 4, core: 2. Of those that a mesh axis runs over, the one named last changes fastest.
Arguments:
- pair_map: bfloat16 [32, 2048, 128], P('row', 'col'), may hold values from -6 to 6
- norm_gain: float32 [128], replicated, may hold values from 0.5 to 1.5
- in_weights: bfloat16 [3, 128, 512], replicated, may hold values from -0.5 to 0.5
- head_gain: float32 [3, 128], replicated, may hold values from 0.5 to 1.5
- out_weights: bfloat16 [3, 128, 128], replicated, may hold values from -0.5 to 0.5
- trans_gain: float32 [128], replicated, may hold values from 0.5 to 1.5
- up_weight: bfloat16 [128, 512], replicated, may hold values from -0.5 to 0.5
- down_weight: bfloat16 [512, 128], replicated, may hold values from -0.25 to 0.25
Outputs:
- result: bfloat16 [32, 2048, 128], P('row', 'col')
The draws below stay inside these ranges and needn't reach their ends.
All inputs are finite; a program needn't handle non-finite values.
Results may differ from the reference program's by a relative error of at most 0.012.
Values may be sent and summed in bfloat16 or wider, within the bound.
No kernel may reach another device: no remote copies, remote signals or barrier semaphores. Data moves between devices by JAX's collectives and lax.ppermute only.
A program may use at most 64 MiB of HBM per device.

```python
import jax
import jax.numpy as jnp
from jax import lax

D = 128
HEADS = 4
HEAD = 32
FF = 512
ROW_DEV = 4
ROWS = 32
COLS = 2048
N_ROW = 8


def block_levels(key, extent, split, low, high):
    loudness = 1.0
    for axis_at, parts in split:
        heights = jax.random.uniform(jax.random.fold_in(jax.random.fold_in(key, 6), axis_at), (parts,), jnp.float32, low / len(split), high / len(split))
        loudness = loudness * jnp.repeat(jnp.exp(heights), extent[axis_at] // parts).reshape((-1,) + (1,) * (len(extent) - 1 - axis_at))
    return loudness


def noise(stream_key, shape, scale, limit, cuts=(), dtype=jnp.bfloat16):
    values = jax.random.normal(stream_key, shape, jnp.float32) * scale
    if len(cuts) > 0:
        values = block_levels(stream_key, shape, cuts, -0.22, 0.18) * values
    return jnp.clip(values, min=-limit, max=limit).astype(dtype)


def setup_inputs(seed: int = 0) -> dict:
    arg_keys = jax.random.split(jax.random.key(seed), 9)
    pair_map = noise(arg_keys[0], (ROWS, COLS, D), 1.0, 6.0, ((0, 8), (1, 4)))
    norm_gain = jnp.clip(1.0 + 0.1 * jax.random.normal(arg_keys[1], (D,), jnp.float32), 0.5, 1.5)
    in_weights = noise(arg_keys[2], (3, D, 4 * D), D ** -0.5, 0.5)
    head_gain = jnp.clip(1.0 + 0.1 * jax.random.normal(arg_keys[3], (3, D), jnp.float32), 0.5, 1.5)
    out_weights = noise(arg_keys[4], (3, D, D), D ** -0.5, 0.5)
    trans_gain = jnp.clip(1.0 + 0.1 * jax.random.normal(arg_keys[5], (D,), jnp.float32), 0.5, 1.5)
    up_weight = noise(arg_keys[6], (D, FF), D ** -0.5, 0.5)
    down_weight = noise(arg_keys[7], (FF, D), FF ** -0.5, 0.25)
    return dict(pair_map=pair_map, norm_gain=norm_gain, in_weights=in_weights, head_gain=head_gain, out_weights=out_weights, trans_gain=trans_gain, up_weight=up_weight, down_weight=down_weight)


epsilon = 1e-05

def feature(values):
    return jnp.where(values > 0, values + 1.0, jnp.exp(jnp.minimum(values, 0.0)))

def normalize(values, gain):
    meansq = lax.optimization_barrier(jnp.mean(values * values, axis=-1, keepdims=True))
    return values * lax.rsqrt(meansq + epsilon) * gain

def open_branch(normed, weight):
    width = weight.shape[0]
    flat = jnp.dot(normed.reshape(-1, width), weight, preferred_element_type=jnp.float32)
    shape = normed.shape[:-1] + (HEADS, HEAD)
    query_feat = feature(flat[:, :width]).astype(jnp.bfloat16).reshape(shape)
    key_feat = feature(flat[:, width:2 * width]).astype(jnp.bfloat16).reshape(shape)
    value_rows = flat[:, 2 * width:3 * width].astype(jnp.bfloat16).reshape(shape)
    gate_vals = jax.nn.sigmoid(flat[:, 3 * width:]).reshape(normed.shape)
    return (query_feat, key_feat, value_rows, gate_vals)

def close_branch(head_out, gate_vals, gain, weight):
    mixed_out = (normalize(head_out.reshape(gate_vals.shape), gain) * gate_vals).astype(jnp.bfloat16)
    width = weight.shape[0]
    projected = jnp.dot(mixed_out.reshape(-1, width), weight, preferred_element_type=jnp.float32)
    return projected.reshape(gate_vals.shape).astype(jnp.bfloat16)

def reference(pair_map, norm_gain, in_weights, head_gain, out_weights, trans_gain, up_weight, down_weight):
    blocks = pair_map.reshape(N_ROW, ROW_DEV, COLS, D)

    def first_pass(column_acc, block):
        normed = normalize(block.astype(jnp.float32), norm_gain).astype(jnp.bfloat16)
        outputs = []
        for branch in range(2):
            query_feat, key_feat, value_rows, gate_vals = open_branch(normed, in_weights[branch])
            states = jnp.einsum('rcha,rchb->rhab', key_feat.astype(jnp.float32), value_rows.astype(jnp.float32)).astype(jnp.bfloat16)
            head_out = jnp.einsum('rcha,rhab->rchb', query_feat.astype(jnp.float32), states.astype(jnp.float32))
            outputs.append(close_branch(head_out, gate_vals, head_gain[branch], out_weights[branch]))
        query_feat, key_feat, value_rows, gate_vals = open_branch(normed, in_weights[2])
        column_acc = column_acc + jnp.einsum('rcha,rchb->chab', key_feat.astype(jnp.float32), value_rows.astype(jnp.float32))
        return (column_acc, (outputs[0], outputs[1]))
    column_zero = jnp.zeros((COLS, HEADS, HEAD, HEAD), jnp.float32)
    column_acc, (first_out, second_out) = lax.scan(first_pass, column_zero, blocks)
    column_states = column_acc.astype(jnp.bfloat16).astype(jnp.float32)

    def second_pass(inputs):
        block, first_rows, second_rows = inputs
        widened = block.astype(jnp.float32)
        normed = normalize(widened, norm_gain).astype(jnp.bfloat16)
        query_feat, key_feat, value_rows, gate_vals = open_branch(normed, in_weights[2])
        head_out = jnp.einsum('rcha,chab->rchb', query_feat.astype(jnp.float32), column_states)
        third_rows = close_branch(head_out, gate_vals, head_gain[2], out_weights[2])
        updated = widened + first_rows.astype(jnp.float32) + second_rows.astype(jnp.float32) + third_rows.astype(jnp.float32)
        trans_in = normalize(updated, trans_gain).astype(jnp.bfloat16)
        hidden = jax.nn.silu(jnp.dot(trans_in.reshape(-1, D), up_weight, preferred_element_type=jnp.float32)).astype(jnp.bfloat16)
        lowered = jnp.dot(hidden, down_weight, preferred_element_type=jnp.float32).reshape(updated.shape)
        return (updated + lowered).astype(jnp.bfloat16)
    result = lax.map(second_pass, (blocks, first_out, second_out))
    return result.reshape(ROWS, COLS, D)
```

```python
import functools

import jax
import jax.numpy as jnp
from jax import lax
from jax.experimental import pallas as pl
from jax.experimental.pallas import tpu as pltpu
from jax.sharding import PartitionSpec as P

HEAD = 32
GROUP = 4
EPSILON = 1e-05
VMEM_LIMIT = 24 * 1024 * 1024

F32 = jnp.float32
BF16 = jnp.bfloat16


def matmul(a, b):
    return jnp.dot(a, b, preferred_element_type=F32)


def matmul_nt(a, b):
    return lax.dot_general(a, b, (((1,), (1,)), ((), ())), preferred_element_type=F32)


def feature(values):
    return jnp.exp(jnp.minimum(values, 0.0)) + jnp.maximum(values, 0.0)


def sigmoid(values):
    return 0.5 * jnp.tanh(0.5 * values) + 0.5


def normalize(values, gain):
    meansq = jnp.mean(values * values, axis=-1, keepdims=True)
    return values * lax.rsqrt(meansq + EPSILON) * gain


def iota(shape, axis):
    return lax.broadcasted_iota(jnp.int32, shape, axis)


def head_mask(rows, width):
    return ((iota((rows, width), 0) % width) // HEAD) == (iota((rows, width), 1) // HEAD)


def interleave(row_count, cols):
    count = row_count * cols
    out = iota((count, count), 0)
    src = iota((count, count), 1)
    hit = (out // row_count == src % cols) & (out % row_count == src // cols)
    return hit.astype(F32).astype(BF16)


def norm_kernel(parts, x_ref, gain_ref, normed_ref, sent_ref):
    row_count, col_count, width = x_ref.shape
    cols = col_count // parts
    order = interleave(row_count, cols)
    gain = gain_ref[...]
    for part in range(parts):
        span = slice(part * cols, (part + 1) * cols)
        block = x_ref[:, span, :].astype(F32).reshape(row_count * cols, width)
        normed = normalize(block, gain).astype(BF16)
        normed_ref[:, span, :] = normed.reshape(row_count, cols, width)
        sent_ref[part] = matmul(order, normed).astype(BF16)


def state_kernel(normed_ref, weight_ref, state_ref):
    row_count, col_count, width = normed_ref.shape
    keep = head_mask(width, width)
    for branch in range(2):
        key_weight = weight_ref[branch, :, width : 2 * width].T
        value_weight = weight_ref[branch, :, 2 * width : 3 * width]
        for row in range(row_count):
            normed = normed_ref[row]
            keys = feature(matmul_nt(key_weight, normed)).astype(BF16)
            values = matmul(normed, value_weight).astype(BF16)
            state = jnp.where(keep, matmul(keys, values), 0.0)
            packed = state[:HEAD]
            for head in range(1, width // HEAD):
                packed = packed + state[head * HEAD : (head + 1) * HEAD]
            state_ref[branch, row] = packed.astype(BF16)


def row_kernel(
    x_ref, normed_ref, state_ref, weight_ref, head_gain_ref, out_weight_ref, updated_ref
):
    row_count, col_count, width = normed_ref.shape
    keep = head_mask(width, width)
    heads = width // HEAD
    for row in range(row_count):
        normed = normed_ref[row]
        total = x_ref[row].astype(F32)
        for branch in range(2):
            packed = state_ref[branch, row].astype(F32)
            state = jnp.where(keep, jnp.concatenate([packed] * heads, axis=0), 0.0).astype(BF16)
            query = feature(matmul(normed, weight_ref[branch, :, :width])).astype(BF16)
            gate = sigmoid(matmul(normed, weight_ref[branch, :, 3 * width :]))
            head_out = matmul(query, state)
            mixed = (normalize(head_out, head_gain_ref[branch : branch + 1]) * gate).astype(BF16)
            total = total + matmul(mixed, out_weight_ref[branch]).astype(BF16).astype(F32)
        updated_ref[row] = total


def column_pass(row_count, got_ref, weight_ref, head_gain_ref, out_weight_ref, sent_ref):
    parts, tokens, width = got_ref.shape
    heads = width // HEAD
    piece = GROUP * row_count
    size = parts * piece
    key_weight = weight_ref[2, :, width : 2 * width].T
    keep = head_mask(GROUP * width, width)
    column_down = (iota((size, width), 0) // row_count) % GROUP
    column_across = (iota((width, size), 1) // row_count) % GROUP
    gain = head_gain_ref[2:3]
    for group in range(tokens // piece):
        span = slice(group * piece, (group + 1) * piece)
        block = jnp.concatenate([got_ref[part, span, :] for part in range(parts)], axis=0)
        keys = feature(matmul_nt(key_weight, block))
        spread_keys = jnp.concatenate(
            [jnp.where(column_across == at, keys, 0.0).astype(BF16) for at in range(GROUP)], axis=0
        )
        values = matmul(block, weight_ref[2, :, 2 * width : 3 * width]).astype(BF16)
        state = jnp.where(keep, matmul(spread_keys, values), 0.0).astype(BF16)
        query = feature(matmul(block, weight_ref[2, :, :width]))
        spread_query = jnp.concatenate(
            [jnp.where(column_down == at, query, 0.0).astype(BF16) for at in range(GROUP)], axis=1
        )
        gate = sigmoid(matmul(block, weight_ref[2, :, 3 * width :]))
        head_out = matmul(spread_query, state)
        mixed = (normalize(head_out, gain) * gate).astype(BF16)
        out = matmul(mixed, out_weight_ref[2]).astype(BF16)
        for part in range(parts):
            sent_ref[part, span, :] = out[part * piece : (part + 1) * piece]


def final_kernel(updated_ref, got_ref, gain_ref, up_ref, down_ref, out_ref):
    row_count, col_count, width = updated_ref.shape
    parts = got_ref.shape[0]
    cols = col_count // parts
    order = interleave(cols, row_count)
    gain = gain_ref[...]
    up = up_ref[...]
    down = down_ref[...]
    for part in range(parts):
        span = slice(part * cols, (part + 1) * cols)
        third = matmul(order, got_ref[part])
        updated = updated_ref[:, span, :].reshape(row_count * cols, width) + third
        trans_in = normalize(updated, gain).astype(BF16)
        hidden = matmul(trans_in, up)
        hidden = (hidden * sigmoid(hidden)).astype(BF16)
        result = (updated + matmul(hidden, down)).astype(BF16)
        out_ref[:, span, :] = result.reshape(row_count, cols, width)


def call(kernel, out_shape, name, flops):
    return pl.pallas_call(
        kernel,
        out_shape=out_shape,
        name=name,
        compiler_params=pltpu.CompilerParams(vmem_limit_bytes=VMEM_LIMIT),
        cost_estimate=pl.CostEstimate(flops=flops, bytes_accessed=1 << 20, transcendentals=0),
    )


def shards(
    parts,
    col_parts,
    pair_map,
    norm_gain,
    in_weights,
    head_gain,
    out_weights,
    trans_gain,
    up_weight,
    down_weight,
):
    row_count, col_count, width = pair_map.shape
    tokens = row_count * (col_count // parts)
    total = row_count * col_count
    struct = jax.ShapeDtypeStruct
    moved = struct((parts, tokens, width), BF16)
    square = total * width * width * 2

    normed, sent = call(
        functools.partial(norm_kernel, parts),
        (struct(pair_map.shape, BF16), moved),
        "norm",
        square,
    )(pair_map, norm_gain.reshape(1, width))
    got = lax.all_to_all(sent, "row", split_axis=0, concat_axis=0, tiled=True)

    state = call(
        state_kernel, struct((2, row_count, HEAD, width), BF16), "row_state", 6 * square
    )(normed, in_weights)
    step = 1
    while step < col_parts:
        pairs = [(at, at ^ step) for at in range(col_parts)]
        state = (state.astype(F32) + lax.ppermute(state, "col", pairs).astype(F32)).astype(BF16)
        step *= 2
    updated = call(row_kernel, struct(pair_map.shape, F32), "row_out", 8 * square)(
        pair_map, normed, state, in_weights, head_gain, out_weights
    )

    column_out = call(
        functools.partial(column_pass, row_count), moved, "column", 10 * square
    )(got, in_weights, head_gain, out_weights)
    third = lax.all_to_all(column_out, "row", split_axis=0, concat_axis=0, tiled=True)

    return call(final_kernel, struct(pair_map.shape, BF16), "final", 9 * square)(
        updated, third, trans_gain.reshape(1, width), up_weight, down_weight
    )


def solution(mesh):
    in_specs = (P("row", "col", None), P(), P(), P(), P(), P(), P(), P())
    out_specs = P("row", "col", None)
    body = functools.partial(shards, mesh.shape["row"], mesh.shape["col"])
    return jax.shard_map(body, mesh=mesh, in_specs=in_specs, out_specs=out_specs, check_vma=False)
```

```python
import functools

import jax
import jax.numpy as jnp
from jax import lax
from jax.experimental import pallas as pl
from jax.experimental.pallas import tpu as pltpu
from jax.sharding import PartitionSpec as P

HEAD = 32
GROUP = 4
EPSILON = 1e-05
CHUNK = 512
VMEM_LIMIT = 24 * 1024 * 1024

F32 = jnp.float32
BF16 = jnp.bfloat16


def matmul(a, b):
    return jnp.dot(a, b, preferred_element_type=F32)


def matmul_nt(a, b):
    return lax.dot_general(a, b, (((1,), (1,)), ((), ())), preferred_element_type=F32)


def feature(values):
    return jnp.exp(jnp.minimum(values, 0.0)) + jnp.maximum(values, 0.0)


def sigmoid(values):
    return 0.5 * jnp.tanh(0.5 * values) + 0.5


def normalize(values, gain):
    meansq = jnp.mean(values * values, axis=-1, keepdims=True)
    return values * lax.rsqrt(meansq + EPSILON) * gain


def iota(shape, axis):
    return lax.broadcasted_iota(jnp.int32, shape, axis)


def head_mask(rows, width):
    return ((iota((rows, width), 0) % width) // HEAD) == (iota((rows, width), 1) // HEAD)


def interleave(row_count, cols):
    count = row_count * cols
    out = iota((count, count), 0)
    src = iota((count, count), 1)
    hit = (out // row_count == src % cols) & (out % row_count == src // cols)
    return hit.astype(F32).astype(BF16)


def norm_kernel(x_ref, gain_ref, normed_ref, *sent_refs):
    row_count, col_count, width = x_ref.shape
    parts = len(sent_refs)
    cols = col_count // parts
    me = lax.axis_index("row")
    order = interleave(row_count, cols)
    gain = gain_ref[:1]
    for step in range(parts):
        span = pl.ds(pl.multiple_of((me ^ step) * cols, cols), cols)
        block = x_ref[:, span, :].astype(F32).reshape(row_count * cols, width)
        normed = normalize(block, gain).astype(BF16)
        normed_ref[:, span, :] = normed.reshape(row_count, cols, width)
        sent_refs[step][...] = matmul(order, normed).astype(BF16)


def state_kernel(normed_ref, weight_ref, after_ref, state_ref):
    row_count, col_count, width = normed_ref.shape
    keep = head_mask(width, width)
    for branch in range(2):
        key_weight = weight_ref[branch, :, width : 2 * width].T
        value_weight = weight_ref[branch, :, 2 * width : 3 * width]
        for row in range(row_count):
            normed = normed_ref[row]
            keys = feature(matmul_nt(key_weight, normed)).astype(BF16)
            values = matmul(normed, value_weight).astype(BF16)
            state = jnp.where(keep, matmul(keys, values), 0.0)
            packed = state[:HEAD]
            for head in range(1, width // HEAD):
                packed = packed + state[head * HEAD : (head + 1) * HEAD]
            state_ref[branch, row] = packed.astype(BF16)


def row_kernel(
    x_ref, normed_ref, state_ref, weight_ref, head_gain_ref, out_weight_ref, gain_ref, updated_ref, gain_out_ref
):
    row_count, col_count, width = normed_ref.shape
    keep = head_mask(width, width)
    heads = width // HEAD
    gain_out_ref[...] = gain_ref[...]
    for row in range(row_count):
        normed = normed_ref[row]
        total = x_ref[row].astype(F32)
        for branch in range(2):
            packed = state_ref[branch, row].astype(F32)
            state = jnp.where(keep, jnp.concatenate([packed] * heads, axis=0), 0.0).astype(BF16)
            query = feature(matmul(normed, weight_ref[branch, :, :width])).astype(BF16)
            gate = sigmoid(matmul(normed, weight_ref[branch, :, 3 * width :]))
            head_out = matmul(query, state)
            mixed = (normalize(head_out, head_gain_ref[branch : branch + 1]) * gate).astype(BF16)
            total = total + matmul(mixed, out_weight_ref[branch]).astype(BF16).astype(F32)
        updated_ref[row] = total


def column_kernel(row_count, order, weight_ref, head_gain_ref, out_weight_ref, *refs):
    parts = len(order)
    got_refs = refs[:parts]
    sent_refs = refs[parts + 1 : 2 * parts + 1]
    block_ref, query_ref, key_ref, value_ref, gate_ref, head_ref = refs[2 * parts + 1 :]
    tokens, width = got_refs[0].shape
    piece = GROUP * row_count
    size = parts * piece
    groups = tokens // piece
    total = parts * tokens
    for step, got_ref in zip(order, got_refs):
        for group in range(groups):
            start = group * size + step * piece
            block_ref[start : start + piece] = got_ref[group * piece : (group + 1) * piece]
    key_weight = weight_ref[2, :, width : 2 * width].T
    for start in range(0, total, CHUNK):
        span = slice(start, start + CHUNK)
        block = block_ref[span]
        query_ref[span] = feature(matmul(block, weight_ref[2, :, :width])).astype(BF16)
        value_ref[span] = matmul(block, weight_ref[2, :, 2 * width : 3 * width]).astype(BF16)
        gate_ref[span] = sigmoid(matmul(block, weight_ref[2, :, 3 * width :]))
        key_ref[:, span] = feature(matmul_nt(key_weight, block)).astype(BF16)
    keep = head_mask(GROUP * width, width).astype(F32).astype(BF16)
    down = (iota((size, width), 0) // row_count) % GROUP
    across = (iota((width, size), 1) // row_count) % GROUP
    down = [(down == at).astype(F32).astype(BF16) for at in range(GROUP)]
    across = [(across == at).astype(F32).astype(BF16) for at in range(GROUP)]
    for group in range(groups):
        span = slice(group * size, (group + 1) * size)
        keys = key_ref[:, span]
        query = query_ref[span]
        spread_keys = jnp.concatenate([keys * mask for mask in across], axis=0)
        state = matmul(spread_keys, value_ref[span]).astype(BF16) * keep
        spread_query = jnp.concatenate([query * mask for mask in down], axis=1)
        head_ref[span] = matmul(spread_query, state)
    gain = head_gain_ref[2:3]
    for start in range(0, total, CHUNK):
        span = slice(start, start + CHUNK)
        mixed = (normalize(head_ref[span], gain) * gate_ref[span]).astype(BF16)
        query_ref[span] = matmul(mixed, out_weight_ref[2]).astype(BF16)
    for step in range(parts):
        for group in range(groups):
            start = group * size + step * piece
            sent_refs[step][group * piece : (group + 1) * piece] = query_ref[start : start + piece]


def final_kernel(steps, parts, fresh, updated_ref, gain_ref, up_ref, down_ref, *refs):
    row_count, col_count, width = updated_ref.shape
    got_refs = refs[: len(steps)]
    out_hbm, sum_ref, trans_ref, hidden_ref, out_ref, sems = refs[len(steps) + (not fresh) :]
    cols = col_count // parts
    tokens = row_count * cols
    me = lax.axis_index("row")
    order = interleave(cols, row_count)
    gain = gain_ref[...]
    spans = [pl.ds(pl.multiple_of((me ^ step) * cols, cols), cols) for step in steps]
    for at, got_ref in enumerate(got_refs):
        span = slice(at * tokens, (at + 1) * tokens)
        third = matmul(order, got_ref[...])
        updated = updated_ref[:, spans[at], :].reshape(tokens, width) + third
        sum_ref[span] = updated
        trans_ref[span] = normalize(updated, gain).astype(BF16)
    for at in range(len(steps)):
        span = slice(at * tokens, (at + 1) * tokens)
        half = 0.5 * matmul(trans_ref[span], up_ref[...])
        hidden_ref[span] = (half * jnp.tanh(half) + half).astype(BF16)
    stores = []
    for at in range(len(steps)):
        span = slice(at * tokens, (at + 1) * tokens)
        result = (sum_ref[span] + matmul(hidden_ref[span], down_ref[...])).astype(BF16)
        out_ref[at] = result.reshape(row_count, cols, width)
        store = pltpu.make_async_copy(out_ref.at[at], out_hbm.at[:, spans[at], :], sems.at[at])
        store.start()
        stores.append(store)
    for store in stores:
        store.wait()


def send_order(parts):
    first = [0, 1, *range(parts // 2, parts), *range(2, parts // 2)]
    return tuple(dict.fromkeys(first[:parts] if parts < 4 else first))


def exchange(pieces):
    parts = len(pieces)
    moved = list(pieces)
    for step in range(parts - 1, 0, -1):
        pairs = [(at, at ^ step) for at in range(parts)]
        moved[step] = lax.ppermute(pieces[step], "row", pairs)
    return moved


def call(kernel, out_shape, name, flops, vmem_limit=VMEM_LIMIT, **kwargs):
    return pl.pallas_call(
        kernel,
        out_shape=out_shape,
        name=name,
        compiler_params=pltpu.CompilerParams(vmem_limit_bytes=vmem_limit),
        cost_estimate=pl.CostEstimate(flops=0, bytes_accessed=0, transcendentals=0),
        **kwargs,
    )


def shards(
    parts,
    col_parts,
    pair_map,
    norm_gain,
    in_weights,
    head_gain,
    out_weights,
    trans_gain,
    up_weight,
    down_weight,
):
    row_count, col_count, width = pair_map.shape
    cols = col_count // parts
    tokens = row_count * cols
    total = row_count * col_count
    hidden = up_weight.shape[1]
    struct = jax.ShapeDtypeStruct
    square = total * width * width * 2
    vmem = pl.BlockSpec(memory_space=pltpu.VMEM)
    anywhere = pl.BlockSpec(memory_space=pl.ANY)

    normed, *sent = call(
        norm_kernel,
        [struct(pair_map.shape, BF16)] + [struct((tokens, width), BF16)] * parts,
        "norm",
        square,
    )(pair_map, jnp.broadcast_to(norm_gain, (8, width)))
    got = exchange(sent)

    state = call(
        state_kernel,
        struct((2, row_count, HEAD, width), BF16),
        "row_state",
        6 * square,
        in_specs=[vmem] * 2 + [anywhere],
    )(normed, in_weights, got[1])
    state0 = state
    step = 1
    while step < col_parts:
        pairs = [(at, at ^ step) for at in range(col_parts)]
        state = (state.astype(F32) + lax.ppermute(state, "col", pairs).astype(F32)).astype(BF16)
        if step == 1:
            state1 = state
        step *= 2
    updated, gain = call(
        row_kernel,
        (struct(pair_map.shape, F32), struct((1, width), F32)),
        "row_out",
        8 * square,
    )(pair_map, normed, state, in_weights, head_gain, out_weights, trans_gain.reshape(1, width))

    order = send_order(parts)
    column_out = call(
        functools.partial(column_kernel, row_count, order),
        [struct((tokens, width), BF16)] * parts,
        "column",
        10 * square,
        in_specs=[vmem] * (3 + parts) + [anywhere],
        scratch_shapes=[
            pltpu.VMEM((total, width), BF16),
            pltpu.VMEM((total, width), BF16),
            pltpu.VMEM((width, total), BF16),
            pltpu.VMEM((total, width), BF16),
            pltpu.VMEM((total, width), F32),
            pltpu.VMEM((total, width), F32),
        ],
    )(in_weights, head_gain, out_weights, *[got[step] for step in order], normed)

    third = exchange(column_out)

    result = None
    for steps in (order,):
        fresh = result is None
        count = len(steps)
        result = call(
            functools.partial(final_kernel, steps, parts, fresh),
            struct(pair_map.shape, BF16),
            "final",
            9 * square * count // parts,
            in_specs=[vmem] * (4 + count) + [anywhere] * (not fresh),
            out_specs=anywhere,
            input_output_aliases={} if fresh else {4 + count: 0},
            scratch_shapes=[
                pltpu.VMEM((count * tokens, width), F32),
                pltpu.VMEM((count * tokens, width), BF16),
                pltpu.VMEM((count * tokens, hidden), BF16),
                pltpu.VMEM((count, row_count, cols, width), BF16),
                pltpu.SemaphoreType.DMA((count,)),
            ],
        )(
            updated,
            gain,
            up_weight,
            down_weight,
            *[third[step] for step in steps],
            *([] if fresh else [result]),
        )
    return result


def solution(mesh):
    in_specs = (P("row", "col", None), P(), P(), P(), P(), P(), P(), P())
    out_specs = P("row", "col", None)
    body = functools.partial(shards, mesh.shape["row"], mesh.shape["col"])
    return jax.shard_map(body, mesh=mesh, in_specs=in_specs, out_specs=out_specs, check_vma=False)
```

```python
import functools

import jax
import jax.numpy as jnp
from jax import lax
from jax.experimental import pallas as pl
from jax.experimental.pallas import tpu as pltpu
from jax.sharding import PartitionSpec as P

HEAD = 32
GROUP = 4
EPSILON = 1e-05
CHUNK = 512
PIECES_FLOPS = 10**10
VMEM_LIMIT = 24 * 1024 * 1024

F32 = jnp.float32
BF16 = jnp.bfloat16


def matmul(a, b):
    return jnp.dot(a, b, preferred_element_type=F32)


def matmul_nt(a, b):
    return lax.dot_general(a, b, (((1,), (1,)), ((), ())), preferred_element_type=F32)


def feature(values):
    return jnp.exp(jnp.minimum(values, 0.0)) + jnp.maximum(values, 0.0)


def sigmoid(values):
    return 0.5 * jnp.tanh(0.5 * values) + 0.5


def normalize(values, gain):
    meansq = jnp.mean(values * values, axis=-1, keepdims=True)
    return values * lax.rsqrt(meansq + EPSILON) * gain


def iota(shape, axis):
    return lax.broadcasted_iota(jnp.int32, shape, axis)


def head_mask(rows, width):
    return ((iota((rows, width), 0) % width) // HEAD) == (iota((rows, width), 1) // HEAD)


def interleave(row_count, cols):
    count = row_count * cols
    out = iota((count, count), 0)
    src = iota((count, count), 1)
    hit = (out // row_count == src % cols) & (out % row_count == src // cols)
    return hit.astype(F32).astype(BF16)


def piece_kernel(x_ref, *sent_refs):
    row_count, col_count, width = x_ref.shape
    parts = len(sent_refs)
    cols = col_count // parts
    me = lax.axis_index("row")
    order = interleave(row_count, cols)
    for step in range(parts):
        span = pl.ds(pl.multiple_of((me ^ step) * cols, cols), cols)
        block = x_ref[:, span, :].reshape(row_count * cols, width)
        sent_refs[step][...] = matmul(order, block).astype(BF16)


def state_kernel(x_ref, gain_ref, weight_ref, after_ref, state_ref, query_ref, gate_ref):
    row_count, col_count, width = x_ref.shape
    keep = head_mask(width, width)
    gain = gain_ref[...]
    for row in range(row_count):
        normed = normalize(x_ref[row].astype(F32), gain).astype(BF16)
        for branch in range(2):
            weight = weight_ref[branch]
            keys = feature(matmul_nt(weight[:, width : 2 * width].T, normed)).astype(BF16)
            values = matmul(normed, weight[:, 2 * width : 3 * width]).astype(BF16)
            state = jnp.where(keep, matmul(keys, values), 0.0)
            packed = state[:HEAD]
            for head in range(1, width // HEAD):
                packed = packed + state[head * HEAD : (head + 1) * HEAD]
            state_ref[branch, row] = packed.astype(BF16)
            query_ref[branch, row] = feature(matmul(normed, weight[:, :width])).astype(BF16)
            gate_ref[branch, row] = sigmoid(matmul(normed, weight[:, 3 * width :]))


def row_kernel(
    x_ref, query_ref, gate_ref, state_ref, head_gain_ref, out_weight_ref, gain_ref, updated_ref, gain_out_ref
):
    row_count, col_count, width = x_ref.shape
    keep = head_mask(width, width)
    heads = width // HEAD
    gain_out_ref[...] = gain_ref[...]
    for row in range(row_count):
        total = x_ref[row].astype(F32)
        for branch in range(2):
            packed = state_ref[branch, row].astype(F32)
            state = jnp.where(keep, jnp.concatenate([packed] * heads, axis=0), 0.0).astype(BF16)
            head_out = matmul(query_ref[branch, row], state)
            mixed = normalize(head_out, head_gain_ref[branch : branch + 1]) * gate_ref[branch, row]
            out = matmul(mixed.astype(BF16), out_weight_ref[branch])
            total = total + out.astype(BF16).astype(F32)
        updated_ref[row] = total


def column_kernel(
    row_count, order, norm_gain_ref, weight_ref, head_gain_ref, out_weight_ref, *refs
):
    parts = len(order)
    got_refs = refs[:parts]
    sent_refs = refs[parts + 1 : 2 * parts + 1]
    block_ref, query_ref, key_ref, value_ref, gate_ref, head_ref = refs[2 * parts + 1 :]
    tokens, width = got_refs[0].shape
    piece = GROUP * row_count
    size = parts * piece
    groups = tokens // piece
    total = parts * tokens
    for step, got_ref in zip(order, got_refs):
        for group in range(groups):
            start = group * size + step * piece
            block_ref[start : start + piece] = got_ref[group * piece : (group + 1) * piece]
    key_weight = weight_ref[2, :, width : 2 * width].T
    for start in range(0, total, CHUNK):
        span = slice(start, start + CHUNK)
        block = normalize(block_ref[span].astype(F32), norm_gain_ref[...]).astype(BF16)
        query_ref[span] = feature(matmul(block, weight_ref[2, :, :width])).astype(BF16)
        value_ref[span] = matmul(block, weight_ref[2, :, 2 * width : 3 * width]).astype(BF16)
        gate_ref[span] = sigmoid(matmul(block, weight_ref[2, :, 3 * width :]))
        key_ref[:, span] = feature(matmul_nt(key_weight, block)).astype(BF16)
    keep = head_mask(GROUP * width, width).astype(F32).astype(BF16)
    down = (iota((size, width), 0) // row_count) % GROUP
    across = (iota((width, size), 1) // row_count) % GROUP
    down = [(down == at).astype(F32).astype(BF16) for at in range(GROUP)]
    across = [(across == at).astype(F32).astype(BF16) for at in range(GROUP)]
    for group in range(groups):
        span = slice(group * size, (group + 1) * size)
        keys = key_ref[:, span]
        query = query_ref[span]
        spread_keys = jnp.concatenate([keys * mask for mask in across], axis=0)
        state = matmul(spread_keys, value_ref[span]).astype(BF16) * keep
        spread_query = jnp.concatenate([query * mask for mask in down], axis=1)
        head_ref[span] = matmul(spread_query, state)
    gain = head_gain_ref[2:3]
    for start in range(0, total, CHUNK):
        span = slice(start, start + CHUNK)
        mixed = (normalize(head_ref[span], gain) * gate_ref[span]).astype(BF16)
        query_ref[span] = matmul(mixed, out_weight_ref[2]).astype(BF16)
    for step in range(parts):
        for group in range(groups):
            start = group * size + step * piece
            sent_refs[step][group * piece : (group + 1) * piece] = query_ref[start : start + piece]


def final_kernel(steps, parts, fresh, updated_ref, gain_ref, up_ref, down_ref, *refs):
    row_count, col_count, width = updated_ref.shape
    got_refs = refs[: len(steps)]
    out_hbm, sum_ref, trans_ref, hidden_ref, out_ref, sems = refs[len(steps) + (not fresh) :]
    cols = col_count // parts
    tokens = row_count * cols
    me = lax.axis_index("row")
    order = interleave(cols, row_count)
    gain = gain_ref[...]
    spans = [pl.ds(pl.multiple_of((me ^ step) * cols, cols), cols) for step in steps]
    for at, got_ref in enumerate(got_refs):
        span = slice(at * tokens, (at + 1) * tokens)
        third = matmul(order, got_ref[...])
        updated = updated_ref[:, spans[at], :].reshape(tokens, width) + third
        sum_ref[span] = updated
        trans_ref[span] = normalize(updated, gain).astype(BF16)
    for at in range(len(steps)):
        span = slice(at * tokens, (at + 1) * tokens)
        half = 0.5 * matmul(trans_ref[span], up_ref[...])
        hidden_ref[span] = (half * jnp.tanh(half) + half).astype(BF16)
    stores = []
    for at in range(len(steps)):
        span = slice(at * tokens, (at + 1) * tokens)
        result = (sum_ref[span] + matmul(hidden_ref[span], down_ref[...])).astype(BF16)
        out_ref[at] = result.reshape(row_count, cols, width)
        store = pltpu.make_async_copy(out_ref.at[at], out_hbm.at[:, spans[at], :], sems.at[at])
        store.start()
        stores.append(store)
    for store in stores:
        store.wait()


def inward_order(parts):
    half = parts // 2
    steps = (0, half, half - 1, *range(half + 1, parts), *range(1, half - 1))
    return tuple(dict.fromkeys(steps))


def outward_orders(parts):
    half = parts // 2
    early = tuple(dict.fromkeys((0, half, 1)))
    late = (*range(half + 1, parts), *range(2, half))
    return (early, late) if late else (early,)


def exchange(pieces):
    parts = len(pieces)
    moved = list(pieces)
    for step in range(parts - 1, 0, -1):
        pairs = [(at, at ^ step) for at in range(parts)]
        moved[step] = lax.ppermute(pieces[step], "row", pairs)
    return moved


def call(kernel, out_shape, name, flops=0, **kwargs):
    return pl.pallas_call(
        kernel,
        out_shape=out_shape,
        name=name,
        compiler_params=pltpu.CompilerParams(vmem_limit_bytes=VMEM_LIMIT),
        cost_estimate=pl.CostEstimate(flops=flops, bytes_accessed=0, transcendentals=0),
        **kwargs,
    )


def shards(
    parts,
    col_parts,
    pair_map,
    norm_gain,
    in_weights,
    head_gain,
    out_weights,
    trans_gain,
    up_weight,
    down_weight,
):
    row_count, col_count, width = pair_map.shape
    cols = col_count // parts
    tokens = row_count * cols
    total = row_count * col_count
    hidden = up_weight.shape[1]
    struct = jax.ShapeDtypeStruct
    vmem = pl.BlockSpec(memory_space=pltpu.VMEM)
    anywhere = pl.BlockSpec(memory_space=pl.ANY)

    sent = call(
        piece_kernel, [struct((tokens, width), BF16)] * parts, "pieces", PIECES_FLOPS
    )(pair_map)
    got = exchange(sent)

    gain_row = norm_gain.reshape(1, width)
    both = (2, *pair_map.shape)
    state, query, gate = call(
        state_kernel,
        (struct((2, row_count, HEAD, width), BF16), struct(both, BF16), struct(both, F32)),
        "row_state",
        in_specs=[vmem] * 3 + [anywhere],
    )(pair_map, gain_row, in_weights, got[parts // 2])
    step = 1
    while step < col_parts:
        pairs = [(at, at ^ step) for at in range(col_parts)]
        state = (state.astype(F32) + lax.ppermute(state, "col", pairs).astype(F32)).astype(BF16)
        step *= 2
    updated, gain = call(
        row_kernel,
        (struct(pair_map.shape, F32), struct((1, width), F32)),
        "row_out",
    )(pair_map, query, gate, state, head_gain, out_weights, trans_gain.reshape(1, width))
    order = inward_order(parts)
    column_out = call(
        functools.partial(column_kernel, row_count, order),
        [struct((tokens, width), BF16)] * parts,
        "column",
        in_specs=[vmem] * (4 + parts) + [anywhere],
        scratch_shapes=[
            pltpu.VMEM((total, width), BF16),
            pltpu.VMEM((total, width), BF16),
            pltpu.VMEM((width, total), BF16),
            pltpu.VMEM((total, width), BF16),
            pltpu.VMEM((total, width), F32),
            pltpu.VMEM((total, width), F32),
        ],
    )(
        gain_row, in_weights, head_gain, out_weights, *[got[step] for step in order], gate
    )

    third = exchange(column_out)

    result = None
    for steps in outward_orders(parts):
        fresh = result is None
        count = len(steps)
        result = call(
            functools.partial(final_kernel, steps, parts, fresh),
            struct(pair_map.shape, BF16),
            "final",
            in_specs=[vmem] * (4 + count) + [anywhere] * (not fresh),
            out_specs=anywhere,
            input_output_aliases={} if fresh else {4 + count: 0},
            scratch_shapes=[
                pltpu.VMEM((count * tokens, width), F32),
                pltpu.VMEM((count * tokens, width), BF16),
                pltpu.VMEM((count * tokens, hidden), BF16),
                pltpu.VMEM((count, row_count, cols, width), BF16),
                pltpu.SemaphoreType.DMA((count,)),
            ],
        )(
            updated,
            gain,
            up_weight,
            down_weight,
            *[third[step] for step in steps],
            *([] if fresh else [result]),
        )
    return result


def solution(mesh):
    in_specs = (P("row", "col", None), P(), P(), P(), P(), P(), P(), P())
    out_specs = P("row", "col", None)
    body = functools.partial(shards, mesh.shape["row"], mesh.shape["col"])
    return jax.shard_map(body, mesh=mesh, in_specs=in_specs, out_specs=out_specs, check_vma=False)
```

```python
import functools

import jax
import jax.numpy as jnp
from jax import lax
from jax.experimental import pallas as pl
from jax.experimental.pallas import tpu as pltpu
from jax.sharding import PartitionSpec as P

HEAD = 32
GROUP = 4
EPSILON = 1e-05
CHUNK = 512
PIECES_FLOPS = 10**10
VMEM_LIMIT = 24 * 1024 * 1024

F32 = jnp.float32
BF16 = jnp.bfloat16


def matmul(a, b):
    return jnp.dot(a, b, preferred_element_type=F32)


def matmul_nt(a, b):
    return lax.dot_general(a, b, (((1,), (1,)), ((), ())), preferred_element_type=F32)


def feature(values):
    return jnp.exp(jnp.minimum(values, 0.0)) + jnp.maximum(values, 0.0)


def sigmoid(values):
    return 0.5 * jnp.tanh(0.5 * values) + 0.5


def normalize(values, gain):
    meansq = jnp.mean(values * values, axis=-1, keepdims=True)
    return values * lax.rsqrt(meansq + EPSILON) * gain


def iota(shape, axis):
    return lax.broadcasted_iota(jnp.int32, shape, axis)


def head_mask(rows, width):
    return ((iota((rows, width), 0) % width) // HEAD) == (iota((rows, width), 1) // HEAD)


def interleave(row_count, cols):
    count = row_count * cols
    out = iota((count, count), 0)
    src = iota((count, count), 1)
    hit = (out // row_count == src % cols) & (out % row_count == src // cols)
    return hit.astype(F32).astype(BF16)


def piece_kernel(x_ref, *sent_refs):
    row_count, col_count, width = x_ref.shape
    parts = len(sent_refs)
    cols = col_count // parts
    me = lax.axis_index("row")
    order = interleave(row_count, cols)
    for step in range(parts):
        span = pl.ds(pl.multiple_of((me ^ step) * cols, cols), cols)
        block = x_ref[:, span, :].reshape(row_count * cols, width)
        sent_refs[step][...] = matmul(order, block).astype(BF16)


def state_kernel(x_ref, gain_ref, weight_ref, after_ref, state_ref, query_ref, gate_ref):
    row_count, col_count, width = x_ref.shape
    keep = head_mask(width, width)
    gain = gain_ref[...]
    for row in range(row_count):
        normed = normalize(x_ref[row].astype(F32), gain).astype(BF16)
        for branch in range(2):
            weight = weight_ref[branch]
            keys = feature(matmul_nt(weight[:, width : 2 * width].T, normed)).astype(BF16)
            values = matmul(normed, weight[:, 2 * width : 3 * width]).astype(BF16)
            state = jnp.where(keep, matmul(keys, values), 0.0)
            packed = state[:HEAD]
            for head in range(1, width // HEAD):
                packed = packed + state[head * HEAD : (head + 1) * HEAD]
            state_ref[branch, row] = packed.astype(BF16)
            query_ref[branch, row] = feature(matmul(normed, weight[:, :width])).astype(BF16)
            gate_ref[branch, row] = sigmoid(matmul(normed, weight[:, 3 * width :]))


def row_kernel(
    x_ref, query_ref, gate_ref, state_ref, head_gain_ref, out_weight_ref, gain_ref, updated_ref, gain_out_ref
):
    row_count, col_count, width = x_ref.shape
    keep = head_mask(width, width)
    heads = width // HEAD
    gain_out_ref[...] = gain_ref[...]
    for row in range(row_count):
        total = x_ref[row].astype(F32)
        for branch in range(2):
            packed = state_ref[branch, row].astype(F32)
            state = jnp.where(keep, jnp.concatenate([packed] * heads, axis=0), 0.0).astype(BF16)
            head_out = matmul(query_ref[branch, row], state)
            mixed = normalize(head_out, head_gain_ref[branch : branch + 1]) * gate_ref[branch, row]
            out = matmul(mixed.astype(BF16), out_weight_ref[branch])
            total = total + out.astype(BF16).astype(F32)
        updated_ref[row] = total


def column_kernel(
    row_count, order, norm_gain_ref, weight_ref, head_gain_ref, out_weight_ref, *refs
):
    parts = len(order)
    got_refs = refs[:parts]
    sent_refs = refs[parts + 1 : 2 * parts + 1]
    block_ref, query_ref, key_ref, value_ref, gate_ref, head_ref = refs[2 * parts + 1 :]
    tokens, width = got_refs[0].shape
    piece = GROUP * row_count
    size = parts * piece
    groups = tokens // piece
    total = parts * tokens
    for step, got_ref in zip(order, got_refs):
        for group in range(groups):
            start = group * size + step * piece
            block_ref[start : start + piece] = got_ref[group * piece : (group + 1) * piece]
    key_weight = weight_ref[2, :, width : 2 * width].T
    for start in range(0, total, CHUNK):
        span = slice(start, start + CHUNK)
        block = normalize(block_ref[span].astype(F32), norm_gain_ref[...]).astype(BF16)
        query_ref[span] = feature(matmul(block, weight_ref[2, :, :width])).astype(BF16)
        value_ref[span] = matmul(block, weight_ref[2, :, 2 * width : 3 * width]).astype(BF16)
        gate_ref[span] = sigmoid(matmul(block, weight_ref[2, :, 3 * width :]))
        key_ref[:, span] = feature(matmul_nt(key_weight, block)).astype(BF16)
    keep = head_mask(GROUP * width, width).astype(F32).astype(BF16)
    down = (iota((size, width), 0) // row_count) % GROUP
    across = (iota((width, size), 1) // row_count) % GROUP
    down = [(down == at).astype(F32).astype(BF16) for at in range(GROUP)]
    across = [(across == at).astype(F32).astype(BF16) for at in range(GROUP)]
    for group in range(groups):
        span = slice(group * size, (group + 1) * size)
        keys = key_ref[:, span]
        query = query_ref[span]
        spread_keys = jnp.concatenate([keys * mask for mask in across], axis=0)
        state = matmul(spread_keys, value_ref[span]).astype(BF16) * keep
        spread_query = jnp.concatenate([query * mask for mask in down], axis=1)
        head_ref[span] = matmul(spread_query, state)
    gain = head_gain_ref[2:3]
    for start in range(0, total, CHUNK):
        span = slice(start, start + CHUNK)
        mixed = (normalize(head_ref[span], gain) * gate_ref[span]).astype(BF16)
        query_ref[span] = matmul(mixed, out_weight_ref[2]).astype(BF16)
    for step in range(parts):
        for group in range(groups):
            start = group * size + step * piece
            sent_refs[step][group * piece : (group + 1) * piece] = query_ref[start : start + piece]


def final_kernel(steps, parts, fresh, updated_ref, gain_ref, up_ref, down_ref, *refs):
    row_count, col_count, width = updated_ref.shape
    got_refs = refs[: len(steps)]
    out_hbm, sum_ref, trans_ref, hidden_ref, out_ref, sems = refs[len(steps) + (not fresh) :]
    cols = col_count // parts
    tokens = row_count * cols
    me = lax.axis_index("row")
    order = interleave(cols, row_count)
    gain = gain_ref[...]
    spans = [pl.ds(pl.multiple_of((me ^ step) * cols, cols), cols) for step in steps]
    for at, got_ref in enumerate(got_refs):
        span = slice(at * tokens, (at + 1) * tokens)
        third = matmul(order, got_ref[...])
        updated = updated_ref[:, spans[at], :].reshape(tokens, width) + third
        sum_ref[span] = updated
        trans_ref[span] = normalize(updated, gain).astype(BF16)
    for at in range(len(steps)):
        span = slice(at * tokens, (at + 1) * tokens)
        half = 0.5 * matmul(trans_ref[span], up_ref[...])
        hidden_ref[span] = (half * jnp.tanh(half) + half).astype(BF16)
    stores = []
    for at in range(len(steps)):
        span = slice(at * tokens, (at + 1) * tokens)
        result = (sum_ref[span] + matmul(hidden_ref[span], down_ref[...])).astype(BF16)
        out_ref[at] = result.reshape(row_count, cols, width)
        store = pltpu.make_async_copy(out_ref.at[at], out_hbm.at[:, spans[at], :], sems.at[at])
        store.start()
        stores.append(store)
    for store in stores:
        store.wait()


def inward_order(parts):
    half = parts // 2
    steps = (0, half, half - 1, *range(half + 1, parts), *range(1, half - 1))
    return tuple(dict.fromkeys(steps))


def outward_orders(parts):
    half = parts // 2
    early = tuple(dict.fromkeys((0, half, half - 1)))
    late = (*range(half + 1, parts), *range(half - 2, 0, -1))
    return (early, late) if late else (early,)


def exchange(pieces):
    parts = len(pieces)
    moved = list(pieces)
    for step in range(parts - 1, 0, -1):
        pairs = [(at, at ^ step) for at in range(parts)]
        moved[step] = lax.ppermute(pieces[step], "row", pairs)
    return moved


def call(kernel, out_shape, name, flops=0, **kwargs):
    return pl.pallas_call(
        kernel,
        out_shape=out_shape,
        name=name,
        compiler_params=pltpu.CompilerParams(vmem_limit_bytes=VMEM_LIMIT),
        cost_estimate=pl.CostEstimate(flops=flops, bytes_accessed=0, transcendentals=0),
        **kwargs,
    )


def shards(
    parts,
    col_parts,
    pair_map,
    norm_gain,
    in_weights,
    head_gain,
    out_weights,
    trans_gain,
    up_weight,
    down_weight,
):
    row_count, col_count, width = pair_map.shape
    cols = col_count // parts
    tokens = row_count * cols
    total = row_count * col_count
    hidden = up_weight.shape[1]
    struct = jax.ShapeDtypeStruct
    vmem = pl.BlockSpec(memory_space=pltpu.VMEM)
    anywhere = pl.BlockSpec(memory_space=pl.ANY)

    sent = call(
        piece_kernel, [struct((tokens, width), BF16)] * parts, "pieces", PIECES_FLOPS
    )(pair_map)
    got = exchange(sent)

    gain_row = norm_gain.reshape(1, width)
    both = (2, *pair_map.shape)
    state, query, gate = call(
        state_kernel,
        (struct((2, row_count, HEAD, width), BF16), struct(both, BF16), struct(both, F32)),
        "row_state",
        in_specs=[vmem] * 3 + [anywhere],
    )(pair_map, gain_row, in_weights, got[parts // 2])
    step = col_parts // 2
    while step > 0:
        pairs = [(at, at ^ step) for at in range(col_parts)]
        state = (state.astype(F32) + lax.ppermute(state, "col", pairs).astype(F32)).astype(BF16)
        step //= 2
    updated, gain = call(
        row_kernel,
        (struct(pair_map.shape, F32), struct((1, width), F32)),
        "row_out",
    )(pair_map, query, gate, state, head_gain, out_weights, trans_gain.reshape(1, width))
    order = inward_order(parts)
    column_out = call(
        functools.partial(column_kernel, row_count, order),
        [struct((tokens, width), BF16)] * parts,
        "column",
        in_specs=[vmem] * (4 + parts) + [anywhere],
        scratch_shapes=[
            pltpu.VMEM((total, width), BF16),
            pltpu.VMEM((total, width), BF16),
            pltpu.VMEM((width, total), BF16),
            pltpu.VMEM((total, width), BF16),
            pltpu.VMEM((total, width), F32),
            pltpu.VMEM((total, width), F32),
        ],
    )(
        gain_row, in_weights, head_gain, out_weights, *[got[step] for step in order], gate
    )

    third = exchange(column_out)

    result = None
    for steps in outward_orders(parts):
        fresh = result is None
        count = len(steps)
        result = call(
            functools.partial(final_kernel, steps, parts, fresh),
            struct(pair_map.shape, BF16),
            "final",
            in_specs=[vmem] * (4 + count) + [anywhere] * (not fresh),
            out_specs=anywhere,
            input_output_aliases={} if fresh else {4 + count: 0},
            scratch_shapes=[
                pltpu.VMEM((count * tokens, width), F32),
                pltpu.VMEM((count * tokens, width), BF16),
                pltpu.VMEM((count * tokens, hidden), BF16),
                pltpu.VMEM((count, row_count, cols, width), BF16),
                pltpu.SemaphoreType.DMA((count,)),
            ],
        )(
            updated,
            gain,
            up_weight,
            down_weight,
            *[third[step] for step in steps],
            *([] if fresh else [result]),
        )
    return result


def solution(mesh):
    in_specs = (P("row", "col", None), P(), P(), P(), P(), P(), P(), P())
    out_specs = P("row", "col", None)
    body = functools.partial(shards, mesh.shape["row"], mesh.shape["col"])
    return jax.shard_map(body, mesh=mesh, in_specs=in_specs, out_specs=out_specs, check_vma=False)
```

```python
import functools

import jax
import jax.numpy as jnp
from jax import lax
from jax.experimental import pallas as pl
from jax.experimental.pallas import tpu as pltpu
from jax.sharding import PartitionSpec as P

HEAD = 32
GROUP = 4
EPSILON = 1e-05
CHUNK = 512
PIECES_FLOPS = 10**10
VMEM_LIMIT = 24 * 1024 * 1024

F32 = jnp.float32
BF16 = jnp.bfloat16


def matmul(a, b):
    return jnp.dot(a, b, preferred_element_type=F32)


def matmul_nt(a, b):
    return lax.dot_general(a, b, (((1,), (1,)), ((), ())), preferred_element_type=F32)


def feature(values):
    return jnp.exp(jnp.minimum(values, 0.0)) + jnp.maximum(values, 0.0)


def sigmoid(values):
    return 0.5 * jnp.tanh(0.5 * values) + 0.5


def normalize(values, gain):
    meansq = jnp.mean(values * values, axis=-1, keepdims=True)
    return values * lax.rsqrt(meansq + EPSILON) * gain


def iota(shape, axis):
    return lax.broadcasted_iota(jnp.int32, shape, axis)


def head_mask(rows, width):
    return ((iota((rows, width), 0) % width) // HEAD) == (iota((rows, width), 1) // HEAD)


def interleave(row_count, cols):
    count = row_count * cols
    out = iota((count, count), 0)
    src = iota((count, count), 1)
    hit = (out // row_count == src % cols) & (out % row_count == src // cols)
    return hit.astype(F32).astype(BF16)


def piece_kernel(x_ref, *sent_refs):
    row_count, col_count, width = x_ref.shape
    parts = len(sent_refs)
    cols = col_count // parts
    me = lax.axis_index("row")
    order = interleave(row_count, cols)
    for step in range(parts):
        span = pl.ds(pl.multiple_of((me ^ step) * cols, cols), cols)
        block = x_ref[:, span, :].reshape(row_count * cols, width)
        sent_refs[step][...] = matmul(order, block).astype(BF16)


def state_kernel(x_ref, gain_ref, weight_ref, after_ref, state_ref, query_ref, gate_ref):
    row_count, col_count, width = x_ref.shape
    keep = head_mask(width, width)
    gain = gain_ref[...]
    for row in range(row_count):
        normed = normalize(x_ref[row].astype(F32), gain).astype(BF16)
        for branch in range(2):
            weight = weight_ref[branch]
            keys = feature(matmul_nt(weight[:, width : 2 * width].T, normed)).astype(BF16)
            values = matmul(normed, weight[:, 2 * width : 3 * width]).astype(BF16)
            state = jnp.where(keep, matmul(keys, values), 0.0)
            packed = state[:HEAD]
            for head in range(1, width // HEAD):
                packed = packed + state[head * HEAD : (head + 1) * HEAD]
            state_ref[branch, row] = packed.astype(BF16)
            query_ref[branch, row] = feature(matmul(normed, weight[:, :width])).astype(BF16)
            gate_ref[branch, row] = sigmoid(matmul(normed, weight[:, 3 * width :]))


def row_kernel(
    steps,
    parts,
    x_ref,
    query_ref,
    gate_ref,
    state_ref,
    head_gain_ref,
    out_weight_ref,
    gain_ref,
    up_ref,
    down_ref,
    *refs,
):
    updated_ref, gain_out_ref, out_hbm, *scratch = refs[len(steps) :]
    row_count, col_count, width = x_ref.shape
    keep = head_mask(width, width)
    heads = width // HEAD
    gain_out_ref[...] = gain_ref[...]
    for row in range(row_count):
        total = x_ref[row].astype(F32)
        for branch in range(2):
            packed = state_ref[branch, row].astype(F32)
            state = jnp.where(keep, jnp.concatenate([packed] * heads, axis=0), 0.0).astype(BF16)
            head_out = matmul(query_ref[branch, row], state)
            mixed = normalize(head_out, head_gain_ref[branch : branch + 1]) * gate_ref[branch, row]
            out = matmul(mixed.astype(BF16), out_weight_ref[branch])
            total = total + out.astype(BF16).astype(F32)
        updated_ref[row] = total
    finish(steps, parts, updated_ref, gain_ref, up_ref, down_ref, refs[: len(steps)], out_hbm, *scratch)


def column_kernel(
    row_count, order, norm_gain_ref, weight_ref, head_gain_ref, out_weight_ref, *refs
):
    parts = len(order)
    got_refs = refs[:parts]
    sent_refs = refs[parts + 1 : 2 * parts + 1]
    block_ref, query_ref, key_ref, value_ref, gate_ref, head_ref = refs[2 * parts + 1 :]
    tokens, width = got_refs[0].shape
    piece = GROUP * row_count
    size = parts * piece
    groups = tokens // piece
    total = parts * tokens
    for step, got_ref in zip(order, got_refs):
        for group in range(groups):
            start = group * size + step * piece
            block_ref[start : start + piece] = got_ref[group * piece : (group + 1) * piece]
    key_weight = weight_ref[2, :, width : 2 * width].T
    for start in range(0, total, CHUNK):
        span = slice(start, start + CHUNK)
        block = normalize(block_ref[span].astype(F32), norm_gain_ref[...]).astype(BF16)
        query_ref[span] = feature(matmul(block, weight_ref[2, :, :width])).astype(BF16)
        value_ref[span] = matmul(block, weight_ref[2, :, 2 * width : 3 * width]).astype(BF16)
        gate_ref[span] = sigmoid(matmul(block, weight_ref[2, :, 3 * width :]))
        key_ref[:, span] = feature(matmul_nt(key_weight, block)).astype(BF16)
    keep = head_mask(GROUP * width, width).astype(F32).astype(BF16)
    down = (iota((size, width), 0) // row_count) % GROUP
    across = (iota((width, size), 1) // row_count) % GROUP
    down = [(down == at).astype(F32).astype(BF16) for at in range(GROUP)]
    across = [(across == at).astype(F32).astype(BF16) for at in range(GROUP)]
    for group in range(groups):
        span = slice(group * size, (group + 1) * size)
        keys = key_ref[:, span]
        query = query_ref[span]
        spread_keys = jnp.concatenate([keys * mask for mask in across], axis=0)
        state = matmul(spread_keys, value_ref[span]).astype(BF16) * keep
        spread_query = jnp.concatenate([query * mask for mask in down], axis=1)
        head_ref[span] = matmul(spread_query, state)
    gain = head_gain_ref[2:3]
    for start in range(0, total, CHUNK):
        span = slice(start, start + CHUNK)
        mixed = (normalize(head_ref[span], gain) * gate_ref[span]).astype(BF16)
        query_ref[span] = matmul(mixed, out_weight_ref[2]).astype(BF16)
    for step in range(parts):
        for group in range(groups):
            start = group * size + step * piece
            sent_refs[step][group * piece : (group + 1) * piece] = query_ref[start : start + piece]


def finish(
    steps,
    parts,
    updated_ref,
    gain_ref,
    up_ref,
    down_ref,
    got_refs,
    out_hbm,
    sum_ref,
    trans_ref,
    hidden_ref,
    out_ref,
    sems,
):
    row_count, col_count, width = updated_ref.shape
    cols = col_count // parts
    tokens = row_count * cols
    me = lax.axis_index("row")
    order = interleave(cols, row_count)
    gain = gain_ref[...]
    spans = [pl.ds(pl.multiple_of((me ^ step) * cols, cols), cols) for step in steps]
    for at, got_ref in enumerate(got_refs):
        span = slice(at * tokens, (at + 1) * tokens)
        third = matmul(order, got_ref[...])
        updated = updated_ref[:, spans[at], :].reshape(tokens, width) + third
        sum_ref[span] = updated
        trans_ref[span] = normalize(updated, gain).astype(BF16)
    half = 0.5 * matmul(trans_ref[...], up_ref[...])
    hidden_ref[...] = (half * jnp.tanh(half) + half).astype(BF16)
    stores = []
    for at in range(len(steps)):
        span = slice(at * tokens, (at + 1) * tokens)
        result = (sum_ref[span] + matmul(hidden_ref[span], down_ref[...])).astype(BF16)
        out_ref[at] = result.reshape(row_count, cols, width)
        store = pltpu.make_async_copy(out_ref.at[at], out_hbm.at[:, spans[at], :], sems.at[at])
        store.start()
        stores.append(store)
    for store in stores:
        store.wait()


def final_kernel(steps, parts, updated_ref, gain_ref, up_ref, down_ref, *refs):
    got_refs = refs[: len(steps)]
    finish(steps, parts, updated_ref, gain_ref, up_ref, down_ref, got_refs, *refs[len(steps) + 1 :])


def far_steps(parts):
    half = parts // 2
    return (*range(half + 1, min(half + 2, parts)), *range(parts - 1, half + 1, -1))


def inward_order(parts):
    half = parts // 2
    steps = (0, half, half - 1, *far_steps(parts), *range(1, half - 1))
    return tuple(dict.fromkeys(steps))


def outward_orders(parts):
    half = parts // 2
    early = tuple(dict.fromkeys((0, half, half - 1)))
    late = (*far_steps(parts), *range(half - 2, 0, -1))
    return early, late


def exchange(pieces):
    parts = len(pieces)
    moved = list(pieces)
    for step in range(parts - 1, 0, -1):
        pairs = [(at, at ^ step) for at in range(parts)]
        moved[step] = lax.ppermute(pieces[step], "row", pairs)
    return moved


def call(kernel, out_shape, name, flops=0, **kwargs):
    return pl.pallas_call(
        kernel,
        out_shape=out_shape,
        name=name,
        compiler_params=pltpu.CompilerParams(vmem_limit_bytes=VMEM_LIMIT),
        cost_estimate=pl.CostEstimate(flops=flops, bytes_accessed=0, transcendentals=0),
        **kwargs,
    )


def shards(
    parts,
    col_parts,
    pair_map,
    norm_gain,
    in_weights,
    head_gain,
    out_weights,
    trans_gain,
    up_weight,
    down_weight,
):
    row_count, col_count, width = pair_map.shape
    cols = col_count // parts
    tokens = row_count * cols
    total = row_count * col_count
    hidden = up_weight.shape[1]
    struct = jax.ShapeDtypeStruct
    vmem = pl.BlockSpec(memory_space=pltpu.VMEM)
    anywhere = pl.BlockSpec(memory_space=pl.ANY)

    sent = call(
        piece_kernel, [struct((tokens, width), BF16)] * parts, "pieces", PIECES_FLOPS
    )(pair_map)
    got = exchange(sent)

    gain_row = norm_gain.reshape(1, width)
    both = (2, *pair_map.shape)
    state, query, gate = call(
        state_kernel,
        (struct((2, row_count, HEAD, width), BF16), struct(both, BF16), struct(both, F32)),
        "row_state",
        in_specs=[vmem] * 3 + [anywhere],
    )(pair_map, gain_row, in_weights, got[parts // 2])
    step = col_parts // 2
    while step > 0:
        pairs = [(at, at ^ step) for at in range(col_parts)]
        state = (state.astype(F32) + lax.ppermute(state, "col", pairs).astype(F32)).astype(BF16)
        step //= 2
    order = inward_order(parts)
    column_out = call(
        functools.partial(column_kernel, row_count, order),
        [struct((tokens, width), BF16)] * parts,
        "column",
        in_specs=[vmem] * (4 + parts) + [anywhere],
        scratch_shapes=[
            pltpu.VMEM((total, width), BF16),
            pltpu.VMEM((total, width), BF16),
            pltpu.VMEM((width, total), BF16),
            pltpu.VMEM((total, width), BF16),
            pltpu.VMEM((total, width), F32),
            pltpu.VMEM((total, width), F32),
        ],
    )(
        gain_row, in_weights, head_gain, out_weights, *[got[step] for step in order], gate
    )

    third = exchange(column_out)

    def scratch(steps):
        count = len(steps)
        return [
            pltpu.VMEM((count * tokens, width), F32),
            pltpu.VMEM((count * tokens, width), BF16),
            pltpu.VMEM((count * tokens, hidden), BF16),
            pltpu.VMEM((count, row_count, cols, width), BF16),
            pltpu.SemaphoreType.DMA((count,)),
        ]

    early, late = outward_orders(parts)
    updated, gain, result = call(
        functools.partial(row_kernel, early, parts),
        (
            struct(pair_map.shape, F32),
            struct((1, width), F32),
            struct(pair_map.shape, BF16),
        ),
        "row_out",
        in_specs=[vmem] * (9 + len(early)),
        out_specs=(vmem, vmem, anywhere),
        scratch_shapes=scratch(early),
    )(
        pair_map,
        query,
        gate,
        state,
        head_gain,
        out_weights,
        trans_gain.reshape(1, width),
        up_weight,
        down_weight,
        *[third[step] for step in early],
    )
    if not late:
        return result
    return call(
        functools.partial(final_kernel, late, parts),
        struct(pair_map.shape, BF16),
        "final",
        in_specs=[vmem] * (4 + len(late)) + [anywhere],
        out_specs=anywhere,
        input_output_aliases={4 + len(late): 0},
        scratch_shapes=scratch(late),
    )(updated, gain, up_weight, down_weight, *[third[step] for step in late], result)


def solution(mesh):
    in_specs = (P("row", "col", None), P(), P(), P(), P(), P(), P(), P())
    out_specs = P("row", "col", None)
    body = functools.partial(shards, mesh.shape["row"], mesh.shape["col"])
    return jax.shard_map(body, mesh=mesh, in_specs=in_specs, out_specs=out_specs, check_vma=False)
```

```python
import functools

import jax
import jax.numpy as jnp
from jax import lax
from jax.experimental import pallas as pl
from jax.experimental.pallas import tpu as pltpu
from jax.sharding import PartitionSpec as P

HEAD = 32
GROUP = 4
EPSILON = 1e-05
CHUNK = 512
PIECES_FLOPS = 10**10
VMEM_LIMIT = 24 * 1024 * 1024

F32 = jnp.float32
BF16 = jnp.bfloat16


def matmul(a, b):
    return jnp.dot(a, b, preferred_element_type=F32)


def matmul_nt(a, b):
    return lax.dot_general(a, b, (((1,), (1,)), ((), ())), preferred_element_type=F32)


def feature(values):
    return jnp.exp(jnp.minimum(values, 0.0)) + jnp.maximum(values, 0.0)


def sigmoid(values):
    return 0.5 * jnp.tanh(0.5 * values) + 0.5


def normalize(values, gain):
    meansq = jnp.mean(values * values, axis=-1, keepdims=True)
    return values * lax.rsqrt(meansq + EPSILON) * gain


def iota(shape, axis):
    return lax.broadcasted_iota(jnp.int32, shape, axis)


def head_mask(rows, width):
    return ((iota((rows, width), 0) % width) // HEAD) == (iota((rows, width), 1) // HEAD)


def interleave(row_count, cols):
    count = row_count * cols
    out = iota((count, count), 0)
    src = iota((count, count), 1)
    hit = (out // row_count == src % cols) & (out % row_count == src // cols)
    return hit.astype(F32).astype(BF16)


def piece_kernel(x_ref, *sent_refs):
    row_count, col_count, width = x_ref.shape
    parts = len(sent_refs)
    cols = col_count // parts
    me = lax.axis_index("row")
    order = interleave(row_count, cols)
    for step in range(parts):
        span = pl.ds(pl.multiple_of((me ^ step) * cols, cols), cols)
        block = x_ref[:, span, :].reshape(row_count * cols, width)
        sent_refs[step][...] = matmul(order, block).astype(BF16)


def state_kernel(x_ref, gain_ref, weight_ref, after_ref, state_ref, query_ref, gate_ref):
    row_count, col_count, width = x_ref.shape
    keep = head_mask(width, width)
    gain = gain_ref[...]
    for row in range(row_count):
        normed = normalize(x_ref[row].astype(F32), gain).astype(BF16)
        for branch in range(2):
            weight = weight_ref[branch]
            keys = feature(matmul_nt(weight[:, width : 2 * width].T, normed)).astype(BF16)
            values = matmul(normed, weight[:, 2 * width : 3 * width]).astype(BF16)
            state = jnp.where(keep, matmul(keys, values), 0.0)
            packed = state[:HEAD]
            for head in range(1, width // HEAD):
                packed = packed + state[head * HEAD : (head + 1) * HEAD]
            state_ref[branch, row] = packed.astype(BF16)
            query_ref[branch, row] = feature(matmul(normed, weight[:, :width])).astype(BF16)
            gate_ref[branch, row] = sigmoid(matmul(normed, weight[:, 3 * width :]))


def row_kernel(
    steps,
    parts,
    x_ref,
    query_ref,
    gate_ref,
    state_ref,
    head_gain_ref,
    out_weight_ref,
    gain_ref,
    up_ref,
    down_ref,
    *refs,
):
    updated_ref, gain_out_ref, out_hbm, *scratch = refs[len(steps) :]
    row_count, col_count, width = x_ref.shape
    keep = head_mask(width, width)
    heads = width // HEAD
    gain_out_ref[...] = gain_ref[...]
    project = out_weight_ref[:2].reshape(2 * width, width)
    for row in range(row_count):
        mixed = []
        for branch in range(2):
            packed = state_ref[branch, row].astype(F32)
            state = jnp.where(keep, jnp.concatenate([packed] * heads, axis=0), 0.0).astype(BF16)
            head_out = matmul(query_ref[branch, row], state)
            head_out = normalize(head_out, head_gain_ref[branch : branch + 1])
            mixed.append((head_out * gate_ref[branch, row]).astype(BF16))
        total = x_ref[row].astype(F32) + matmul(jnp.concatenate(mixed, axis=1), project)
        updated_ref[row] = total
    finish(steps, parts, updated_ref, gain_ref, up_ref, down_ref, refs[: len(steps)], out_hbm, *scratch)


def column_kernel(
    row_count, order, norm_gain_ref, weight_ref, head_gain_ref, out_weight_ref, *refs
):
    parts = len(order)
    got_refs = refs[:parts]
    sent_refs = refs[parts + 1 : 2 * parts + 1]
    block_ref, query_ref, key_ref, value_ref, gate_ref, head_ref = refs[2 * parts + 1 :]
    tokens, width = got_refs[0].shape
    piece = GROUP * row_count
    size = parts * piece
    groups = tokens // piece
    total = parts * tokens
    for step, got_ref in zip(order, got_refs):
        for group in range(groups):
            start = group * size + step * piece
            block_ref[start : start + piece] = got_ref[group * piece : (group + 1) * piece]
    key_weight = weight_ref[2, :, width : 2 * width].T
    for start in range(0, total, CHUNK):
        span = slice(start, start + CHUNK)
        block = normalize(block_ref[span].astype(F32), norm_gain_ref[...]).astype(BF16)
        query_ref[span] = feature(matmul(block, weight_ref[2, :, :width])).astype(BF16)
        value_ref[span] = matmul(block, weight_ref[2, :, 2 * width : 3 * width]).astype(BF16)
        gate_ref[span] = sigmoid(matmul(block, weight_ref[2, :, 3 * width :]))
        key_ref[:, span] = feature(matmul_nt(key_weight, block)).astype(BF16)
    keep = head_mask(GROUP * width, width).astype(F32).astype(BF16)
    down = (iota((size, width), 0) // row_count) % GROUP
    across = (iota((width, size), 1) // row_count) % GROUP
    down = [(down == at).astype(F32).astype(BF16) for at in range(GROUP)]
    across = [(across == at).astype(F32).astype(BF16) for at in range(GROUP)]
    for group in range(groups):
        span = slice(group * size, (group + 1) * size)
        keys = key_ref[:, span]
        query = query_ref[span]
        spread_keys = jnp.concatenate([keys * mask for mask in across], axis=0)
        state = matmul(spread_keys, value_ref[span]).astype(BF16) * keep
        spread_query = jnp.concatenate([query * mask for mask in down], axis=1)
        head_ref[span] = matmul(spread_query, state)
    gain = head_gain_ref[2:3]
    for start in range(0, total, CHUNK):
        span = slice(start, start + CHUNK)
        mixed = (normalize(head_ref[span], gain) * gate_ref[span]).astype(BF16)
        query_ref[span] = matmul(mixed, out_weight_ref[2]).astype(BF16)
    for step in range(parts):
        for group in range(groups):
            start = group * size + step * piece
            sent_refs[step][group * piece : (group + 1) * piece] = query_ref[start : start + piece]


def finish(
    steps,
    parts,
    updated_ref,
    gain_ref,
    up_ref,
    down_ref,
    got_refs,
    out_hbm,
    sum_ref,
    trans_ref,
    hidden_ref,
    out_ref,
    sems,
):
    row_count, col_count, width = updated_ref.shape
    cols = col_count // parts
    tokens = row_count * cols
    me = lax.axis_index("row")
    order = interleave(cols, row_count)
    gain = gain_ref[...]
    spans = [pl.ds(pl.multiple_of((me ^ step) * cols, cols), cols) for step in steps]
    for at, got_ref in enumerate(got_refs):
        span = slice(at * tokens, (at + 1) * tokens)
        third = matmul(order, got_ref[...])
        updated = updated_ref[:, spans[at], :].reshape(tokens, width) + third
        sum_ref[span] = updated
        trans_ref[span] = normalize(updated, gain).astype(BF16)
    half = 0.5 * matmul(trans_ref[...], up_ref[...])
    hidden_ref[...] = (half * jnp.tanh(half) + half).astype(BF16)
    stores = []
    for at in range(len(steps)):
        span = slice(at * tokens, (at + 1) * tokens)
        result = (sum_ref[span] + matmul(hidden_ref[span], down_ref[...])).astype(BF16)
        out_ref[at] = result.reshape(row_count, cols, width)
        store = pltpu.make_async_copy(out_ref.at[at], out_hbm.at[:, spans[at], :], sems.at[at])
        store.start()
        stores.append(store)
    for store in stores:
        store.wait()


def final_kernel(steps, parts, updated_ref, gain_ref, up_ref, down_ref, *refs):
    got_refs = refs[: len(steps)]
    finish(steps, parts, updated_ref, gain_ref, up_ref, down_ref, got_refs, *refs[len(steps) + 1 :])


def far_steps(parts):
    half = parts // 2
    return (*range(half + 1, min(half + 2, parts)), *range(parts - 1, half + 1, -1))


def inward_order(parts):
    half = parts // 2
    steps = (0, half, half - 1, *far_steps(parts), *range(1, half - 1))
    return tuple(dict.fromkeys(steps))


def outward_orders(parts):
    half = parts // 2
    early = tuple(dict.fromkeys((0, half, half - 1)))
    late = (*far_steps(parts), *range(half - 2, 0, -1))
    return early, late


def exchange(pieces):
    parts = len(pieces)
    moved = list(pieces)
    for step in range(parts - 1, 0, -1):
        pairs = [(at, at ^ step) for at in range(parts)]
        moved[step] = lax.ppermute(pieces[step], "row", pairs)
    return moved


def call(kernel, out_shape, name, flops=0, **kwargs):
    return pl.pallas_call(
        kernel,
        out_shape=out_shape,
        name=name,
        compiler_params=pltpu.CompilerParams(vmem_limit_bytes=VMEM_LIMIT),
        cost_estimate=pl.CostEstimate(flops=flops, bytes_accessed=0, transcendentals=0),
        **kwargs,
    )


def shards(
    parts,
    col_parts,
    pair_map,
    norm_gain,
    in_weights,
    head_gain,
    out_weights,
    trans_gain,
    up_weight,
    down_weight,
):
    row_count, col_count, width = pair_map.shape
    cols = col_count // parts
    tokens = row_count * cols
    total = row_count * col_count
    hidden = up_weight.shape[1]
    struct = jax.ShapeDtypeStruct
    vmem = pl.BlockSpec(memory_space=pltpu.VMEM)
    anywhere = pl.BlockSpec(memory_space=pl.ANY)

    sent = call(
        piece_kernel, [struct((tokens, width), BF16)] * parts, "pieces", PIECES_FLOPS
    )(pair_map)
    got = exchange(sent)

    gain_row = norm_gain.reshape(1, width)
    both = (2, *pair_map.shape)
    state, query, gate = call(
        state_kernel,
        (struct((2, row_count, HEAD, width), BF16), struct(both, BF16), struct(both, F32)),
        "row_state",
        in_specs=[vmem] * 3 + [anywhere],
    )(pair_map, gain_row, in_weights, got[parts // 2])
    step = col_parts // 2
    while step > 0:
        pairs = [(at, at ^ step) for at in range(col_parts)]
        state = (state.astype(F32) + lax.ppermute(state, "col", pairs).astype(F32)).astype(BF16)
        step //= 2
    order = inward_order(parts)
    column_out = call(
        functools.partial(column_kernel, row_count, order),
        [struct((tokens, width), BF16)] * parts,
        "column",
        in_specs=[vmem] * (4 + parts) + [anywhere],
        scratch_shapes=[
            pltpu.VMEM((total, width), BF16),
            pltpu.VMEM((total, width), BF16),
            pltpu.VMEM((width, total), BF16),
            pltpu.VMEM((total, width), BF16),
            pltpu.VMEM((total, width), F32),
            pltpu.VMEM((total, width), F32),
        ],
    )(
        gain_row, in_weights, head_gain, out_weights, *[got[step] for step in order], gate
    )

    third = exchange(column_out)

    def scratch(steps):
        count = len(steps)
        return [
            pltpu.VMEM((count * tokens, width), F32),
            pltpu.VMEM((count * tokens, width), BF16),
            pltpu.VMEM((count * tokens, hidden), BF16),
            pltpu.VMEM((count, row_count, cols, width), BF16),
            pltpu.SemaphoreType.DMA((count,)),
        ]

    early, late = outward_orders(parts)
    updated, gain, result = call(
        functools.partial(row_kernel, early, parts),
        (
            struct(pair_map.shape, F32),
            struct((1, width), F32),
            struct(pair_map.shape, BF16),
        ),
        "row_out",
        in_specs=[vmem] * (9 + len(early)),
        out_specs=(vmem, vmem, anywhere),
        scratch_shapes=scratch(early),
    )(
        pair_map,
        query,
        gate,
        state,
        head_gain,
        out_weights,
        trans_gain.reshape(1, width),
        up_weight,
        down_weight,
        *[third[step] for step in early],
    )
    if not late:
        return result
    return call(
        functools.partial(final_kernel, late, parts),
        struct(pair_map.shape, BF16),
        "final",
        in_specs=[vmem] * (4 + len(late)) + [anywhere],
        out_specs=anywhere,
        input_output_aliases={4 + len(late): 0},
        scratch_shapes=scratch(late),
    )(updated, gain, up_weight, down_weight, *[third[step] for step in late], result)


def solution(mesh):
    in_specs = (P("row", "col", None), P(), P(), P(), P(), P(), P(), P())
    out_specs = P("row", "col", None)
    body = functools.partial(shards, mesh.shape["row"], mesh.shape["col"])
    return jax.shard_map(body, mesh=mesh, in_specs=in_specs, out_specs=out_specs, check_vma=False)
```

```python
import functools

import jax
import jax.numpy as jnp
from jax import lax
from jax.experimental import pallas as pl
from jax.experimental.pallas import tpu as pltpu
from jax.sharding import PartitionSpec as P

HEAD = 32
GROUP = 4
EPSILON = 1e-05
CHUNK = 512
PIECES_FLOPS = 10**10
VMEM_LIMIT = 24 * 1024 * 1024

F32 = jnp.float32
BF16 = jnp.bfloat16


def matmul(a, b):
    return jnp.dot(a, b, preferred_element_type=F32)


def matmul_nt(a, b):
    return lax.dot_general(a, b, (((1,), (1,)), ((), ())), preferred_element_type=F32)


def feature(values):
    return jnp.exp(jnp.minimum(values, 0.0)) + jnp.maximum(values, 0.0)


def sigmoid(values):
    return 0.5 * jnp.tanh(0.5 * values) + 0.5


def normalize(values, gain):
    meansq = jnp.mean(values * values, axis=-1, keepdims=True)
    return values * lax.rsqrt(meansq + EPSILON) * gain


def iota(shape, axis):
    return lax.broadcasted_iota(jnp.int32, shape, axis)


def head_mask(rows, width):
    return ((iota((rows, width), 0) % width) // HEAD) == (iota((rows, width), 1) // HEAD)


def interleave(row_count, cols):
    count = row_count * cols
    out = iota((count, count), 0)
    src = iota((count, count), 1)
    hit = (out // row_count == src % cols) & (out % row_count == src // cols)
    return hit.astype(F32).astype(BF16)


def piece_kernel(x_ref, *sent_refs):
    row_count, col_count, width = x_ref.shape
    parts = len(sent_refs)
    cols = col_count // parts
    me = lax.axis_index("row")
    order = interleave(row_count, cols)
    for step in range(parts):
        span = pl.ds(pl.multiple_of((me ^ step) * cols, cols), cols)
        block = x_ref[:, span, :].reshape(row_count * cols, width)
        sent_refs[step][...] = matmul(order, block).astype(BF16)


def state_kernel(x_ref, gain_ref, weight_ref, after_ref, state_ref, query_ref, gate_ref):
    row_count, col_count, width = x_ref.shape
    keep = head_mask(width, width)
    gain = gain_ref[...]
    for row in range(row_count):
        normed = normalize(x_ref[row].astype(F32), gain).astype(BF16)
        for branch in range(2):
            weight = weight_ref[branch]
            keys = feature(matmul_nt(weight[:, width : 2 * width].T, normed)).astype(BF16)
            values = matmul(normed, weight[:, 2 * width : 3 * width]).astype(BF16)
            state = jnp.where(keep, matmul(keys, values), 0.0)
            packed = state[:HEAD]
            for head in range(1, width // HEAD):
                packed = packed + state[head * HEAD : (head + 1) * HEAD]
            state_ref[branch, row] = packed.astype(BF16)
            query_ref[branch, row] = feature(matmul(normed, weight[:, :width])).astype(BF16)
            gate_ref[branch, row] = sigmoid(matmul(normed, weight[:, 3 * width :]))


def row_kernel(
    steps,
    parts,
    x_ref,
    query_ref,
    gate_ref,
    state_ref,
    head_gain_ref,
    out_weight_ref,
    gain_ref,
    up_ref,
    down_ref,
    *refs,
):
    updated_ref, gain_out_ref, out_hbm, *scratch = refs[len(steps) :]
    row_count, col_count, width = x_ref.shape
    keep = head_mask(width, width)
    heads = width // HEAD
    gain_out_ref[...] = gain_ref[...]
    for row in range(row_count):
        total = x_ref[row].astype(F32)
        for branch in range(2):
            packed = state_ref[branch, row].astype(F32)
            state = jnp.where(keep, jnp.concatenate([packed] * heads, axis=0), 0.0).astype(BF16)
            head_out = matmul(query_ref[branch, row], state)
            mixed = normalize(head_out, head_gain_ref[branch : branch + 1]) * gate_ref[branch, row]
            out = matmul(mixed.astype(BF16), out_weight_ref[branch])
            total = total + out.astype(BF16).astype(F32)
        updated_ref[row] = total
    finish(steps, parts, updated_ref, gain_ref, up_ref, down_ref, refs[: len(steps)], out_hbm, *scratch)


def column_kernel(
    row_count, order, norm_gain_ref, weight_ref, head_gain_ref, out_weight_ref, *refs
):
    parts = len(order)
    got_refs = refs[:parts]
    sent_refs = refs[parts + 1 : 2 * parts + 1]
    block_ref, query_ref, key_ref, value_ref, gate_ref, head_ref = refs[2 * parts + 1 :]
    tokens, width = got_refs[0].shape
    piece = GROUP * row_count
    size = parts * piece
    groups = tokens // piece
    total = parts * tokens
    for step, got_ref in zip(order, got_refs):
        for group in range(groups):
            start = group * size + step * piece
            block_ref[start : start + piece] = got_ref[group * piece : (group + 1) * piece]
    key_weight = weight_ref[2, :, width : 2 * width].T
    for start in range(0, total, CHUNK):
        span = slice(start, start + CHUNK)
        block = normalize(block_ref[span].astype(F32), norm_gain_ref[...]).astype(BF16)
        query_ref[span] = feature(matmul(block, weight_ref[2, :, :width])).astype(BF16)
        value_ref[span] = matmul(block, weight_ref[2, :, 2 * width : 3 * width]).astype(BF16)
        gate_ref[span] = sigmoid(matmul(block, weight_ref[2, :, 3 * width :]))
        key_ref[:, span] = feature(matmul_nt(key_weight, block)).astype(BF16)
    keep = head_mask(GROUP * width, width).astype(F32).astype(BF16)
    down = (iota((size, width), 0) // row_count) % GROUP
    across = (iota((width, size), 1) // row_count) % GROUP
    down = [(down == at).astype(F32).astype(BF16) for at in range(GROUP)]
    across = [(across == at).astype(F32).astype(BF16) for at in range(GROUP)]
    for group in range(groups):
        span = slice(group * size, (group + 1) * size)
        keys = key_ref[:, span]
        query = query_ref[span]
        spread_keys = jnp.concatenate([keys * mask for mask in across], axis=0)
        state = matmul(spread_keys, value_ref[span]).astype(BF16) * keep
        spread_query = jnp.concatenate([query * mask for mask in down], axis=1)
        head_ref[span] = matmul(spread_query, state)
    gain = head_gain_ref[2:3]
    for start in range(0, total, CHUNK):
        span = slice(start, start + CHUNK)
        mixed = (normalize(head_ref[span], gain) * gate_ref[span]).astype(BF16)
        query_ref[span] = matmul(mixed, out_weight_ref[2]).astype(BF16)
    for step in range(parts):
        for group in range(groups):
            start = group * size + step * piece
            sent_refs[step][group * piece : (group + 1) * piece] = query_ref[start : start + piece]


def finish(
    steps,
    parts,
    updated_ref,
    gain_ref,
    up_ref,
    down_ref,
    got_refs,
    out_hbm,
    sum_ref,
    trans_ref,
    hidden_ref,
    out_ref,
    sems,
):
    row_count, col_count, width = updated_ref.shape
    cols = col_count // parts
    tokens = row_count * cols
    me = lax.axis_index("row")
    order = interleave(cols, row_count)
    gain = gain_ref[...]
    spans = [pl.ds(pl.multiple_of((me ^ step) * cols, cols), cols) for step in steps]
    for at, got_ref in enumerate(got_refs):
        span = slice(at * tokens, (at + 1) * tokens)
        third = matmul(order, got_ref[...])
        updated = updated_ref[:, spans[at], :].reshape(tokens, width) + third
        sum_ref[span] = updated
        trans_ref[span] = normalize(updated, gain).astype(BF16)
    half = 0.5 * matmul(trans_ref[...], up_ref[...])
    hidden_ref[...] = (half * jnp.tanh(half) + half).astype(BF16)
    stores = []
    for at in range(len(steps)):
        span = slice(at * tokens, (at + 1) * tokens)
        result = (sum_ref[span] + matmul(hidden_ref[span], down_ref[...])).astype(BF16)
        out_ref[at] = result.reshape(row_count, cols, width)
        store = pltpu.make_async_copy(out_ref.at[at], out_hbm.at[:, spans[at], :], sems.at[at])
        store.start()
        stores.append(store)
    for store in stores:
        store.wait()


def final_kernel(steps, parts, updated_ref, gain_ref, up_ref, down_ref, *refs):
    got_refs = refs[: len(steps)]
    finish(steps, parts, updated_ref, gain_ref, up_ref, down_ref, got_refs, *refs[len(steps) + 1 :])


def far_steps(parts):
    half = parts // 2
    return (*range(half + 1, min(half + 2, parts)), *range(parts - 1, half + 1, -1))


def inward_order(parts):
    half = parts // 2
    steps = (0, half, half - 1, parts - 1, *range(half + 1, parts - 1), *range(half - 2, 0, -1))
    return tuple(dict.fromkeys(steps))


def outward_orders(parts):
    half = parts // 2
    early = tuple(dict.fromkeys((0, half, half - 1)))
    late = (*far_steps(parts), *range(half - 2, 0, -1))
    return early, late


def exchange(pieces):
    parts = len(pieces)
    moved = list(pieces)
    for step in range(parts - 1, 0, -1):
        pairs = [(at, at ^ step) for at in range(parts)]
        moved[step] = lax.ppermute(pieces[step], "row", pairs)
    return moved


def call(kernel, out_shape, name, flops=0, **kwargs):
    return pl.pallas_call(
        kernel,
        out_shape=out_shape,
        name=name,
        compiler_params=pltpu.CompilerParams(vmem_limit_bytes=VMEM_LIMIT),
        cost_estimate=pl.CostEstimate(flops=flops, bytes_accessed=0, transcendentals=0),
        **kwargs,
    )


def shards(
    parts,
    col_parts,
    pair_map,
    norm_gain,
    in_weights,
    head_gain,
    out_weights,
    trans_gain,
    up_weight,
    down_weight,
):
    row_count, col_count, width = pair_map.shape
    cols = col_count // parts
    tokens = row_count * cols
    total = row_count * col_count
    hidden = up_weight.shape[1]
    struct = jax.ShapeDtypeStruct
    vmem = pl.BlockSpec(memory_space=pltpu.VMEM)
    anywhere = pl.BlockSpec(memory_space=pl.ANY)

    sent = call(
        piece_kernel, [struct((tokens, width), BF16)] * parts, "pieces", PIECES_FLOPS
    )(pair_map)
    got = exchange(sent)

    gain_row = norm_gain.reshape(1, width)
    both = (2, *pair_map.shape)
    state, query, gate = call(
        state_kernel,
        (struct((2, row_count, HEAD, width), BF16), struct(both, BF16), struct(both, F32)),
        "row_state",
        in_specs=[vmem] * 3 + [anywhere],
    )(pair_map, gain_row, in_weights, got[parts // 2])
    step = col_parts // 2
    while step > 0:
        pairs = [(at, at ^ step) for at in range(col_parts)]
        state = (state.astype(F32) + lax.ppermute(state, "col", pairs).astype(F32)).astype(BF16)
        step //= 2
    order = inward_order(parts)
    column_out = call(
        functools.partial(column_kernel, row_count, order),
        [struct((tokens, width), BF16)] * parts,
        "column",
        in_specs=[vmem] * (4 + parts) + [anywhere],
        scratch_shapes=[
            pltpu.VMEM((total, width), BF16),
            pltpu.VMEM((total, width), BF16),
            pltpu.VMEM((width, total), BF16),
            pltpu.VMEM((total, width), BF16),
            pltpu.VMEM((total, width), F32),
            pltpu.VMEM((total, width), F32),
        ],
    )(
        gain_row, in_weights, head_gain, out_weights, *[got[step] for step in order], gate
    )

    third = exchange(column_out)

    def scratch(steps):
        count = len(steps)
        return [
            pltpu.VMEM((count * tokens, width), F32),
            pltpu.VMEM((count * tokens, width), BF16),
            pltpu.VMEM((count * tokens, hidden), BF16),
            pltpu.VMEM((count, row_count, cols, width), BF16),
            pltpu.SemaphoreType.DMA((count,)),
        ]

    early, late = outward_orders(parts)
    updated, gain, result = call(
        functools.partial(row_kernel, early, parts),
        (
            struct(pair_map.shape, F32),
            struct((1, width), F32),
            struct(pair_map.shape, BF16),
        ),
        "row_out",
        in_specs=[vmem] * (9 + len(early)),
        out_specs=(vmem, vmem, anywhere),
        scratch_shapes=scratch(early),
    )(
        pair_map,
        query,
        gate,
        state,
        head_gain,
        out_weights,
        trans_gain.reshape(1, width),
        up_weight,
        down_weight,
        *[third[step] for step in early],
    )
    if not late:
        return result
    return call(
        functools.partial(final_kernel, late, parts),
        struct(pair_map.shape, BF16),
        "final",
        in_specs=[vmem] * (4 + len(late)) + [anywhere],
        out_specs=anywhere,
        input_output_aliases={4 + len(late): 0},
        scratch_shapes=scratch(late),
    )(updated, gain, up_weight, down_weight, *[third[step] for step in late], result)


def solution(mesh):
    in_specs = (P("row", "col", None), P(), P(), P(), P(), P(), P(), P())
    out_specs = P("row", "col", None)
    body = functools.partial(shards, mesh.shape["row"], mesh.shape["col"])
    return jax.shard_map(body, mesh=mesh, in_specs=in_specs, out_specs=out_specs, check_vma=False)
```
